1024 devices in a mesh: dp: 32 (over z_lo, x), expert: 32 (over z_hi, y, core).
Axes of the slice: x: 8, y: 8, z: 8 (z_hi: 2, z_lo: 4; z = z_hi * 4 + z_lo), core: 2. Of those that a mesh axis runs over, the one named last changes fastest.
Arguments:
- tokens: bfloat16 [4096, 2048], P('expert'), may hold values from -6 to 6
- expert_ids: int32 [4096], P('expert'), may hold values from 0 to 31, as said below
- w_router: bfloat16 [2048, 32], replicated, may hold values from -0.125 to 0.125
- w_gate: bfloat16 [32, 2048, 8192], P('expert', None, 'dp'), may hold values from -0.125 to 0.125
- w_up: bfloat16 [32, 2048, 8192], P('expert', None, 'dp'), may hold values from -0.125 to 0.125
- w_down: bfloat16 [32, 8192, 2048], P('expert', 'dp'), may hold values from -0.125 to 0.125
Outputs:
- moe_out: bfloat16 [4096, 2048], P('expert', 'dp')
The draws below stay inside these ranges and needn't reach their ends.
Inputs may be any that keep to these rules, and one draw needn't show every extreme that they name: `expert_ids`: within each block of 128 consecutive tokens no expert is named more than 12 times; one expert, the same for all blocks, is named exactly 12 times in every block.
All inputs are finite; a program needn't handle non-finite values.
Results may differ from the reference program's by a relative error of at most 0.0057.
Values may be sent and summed in bfloat16 or wider, within the bound.
A program may use at most 64 MiB of HBM per device.

```python
import jax
import jax.numpy as jnp
from jax import lax

D = 2048
FF = 8192
TOK_COL = 128
EXPERTS = 32
CAP = 12
TOKENS = 4096


def draw_expert_ids(key, part):
    key_special, key_columns = jax.random.split(jax.random.fold_in(key, 17))
    special = jax.random.randint(key_special, (), 0, EXPERTS).astype(jnp.int32)

    def one_column(column_key):
        first_key, second_key = jax.random.split(column_key)
        pool = (jnp.arange((EXPERTS - 1) * CAP, dtype=jnp.int32) // CAP).astype(jnp.int32)
        chosen = jax.random.permutation(first_key, pool)[:TOK_COL - CAP]
        others = chosen + (chosen >= special).astype(jnp.int32)
        full_ids = jnp.concatenate([jnp.full((CAP,), special, jnp.int32), others])
        return jax.random.permutation(second_key, full_ids)
    column_keys = jax.random.split(key_columns, TOKENS // TOK_COL)
    return jax.vmap(one_column)(column_keys).reshape(TOKENS).astype(jnp.int32)


def raised(entries, own_key, source, target, blocks, factor):
    owner, partner = [(jnp.arange(entries.shape[axis_at]) // (entries.shape[axis_at] // blocks)).reshape([-1 if axis == axis_at else 1 for axis in range(entries.ndim)]) for axis_at in (source, target)]
    chosen = jax.random.permutation(own_key, blocks)[partner]
    strong = (owner == chosen) | (owner == (partner + blocks // 2) % blocks)
    return jnp.where(strong, factor * entries, entries)


def shard_levels(key, shape, shards, low, largest):
    level, own = 1.0, jax.random.fold_in(key, 6)
    for axis_at, blocks in shards:
        heights = jnp.exp(jax.random.uniform(jax.random.fold_in(own, axis_at), (blocks,), jnp.float32, low / len(shards), largest / len(shards)))
        level = level * jnp.repeat(heights, shape[axis_at] // blocks).reshape([-1 if axis == axis_at else 1 for axis in range(len(shape))])
    return level


def gaussian(rng, shape, width, most, cuts=(), kind=jnp.bfloat16):
    entries = jax.random.normal(rng, shape, jnp.float32) * width
    if len(cuts) > 0:
        entries = shard_levels(rng, shape, cuts, -0.22, 0.18) * entries
    return jnp.clip(entries, min=-most, max=most).astype(kind)


def noise_with(rng, shape, deviation, reach, shards, heavy, kind=jnp.bfloat16):
    result = deviation * jax.random.normal(rng, shape, jnp.float32)
    if shards:
        result = result * shard_levels(rng, shape, shards, -0.22, 0.18)
    return jnp.clip(raised(result, jax.random.fold_in(rng, 3), *heavy), -reach, reach).astype(kind)


def setup_inputs(seed: int = 0) -> dict:
    seeds = jax.random.split(jax.random.key(seed), 7)
    return {
        "tokens": gaussian(seeds[0], (TOKENS, D), 1.0, 6.0, ((0, 32),)),
        "expert_ids": draw_expert_ids(jax.random.fold_in(seeds[6], 71), 0),
        "w_router": gaussian(seeds[2], (D, EXPERTS), D ** -0.5, 0.125),
        "w_gate": gaussian(seeds[3], (EXPERTS, D, FF), D ** -0.5, 0.125, ((0, 32), (2, 32))),
        "w_up": gaussian(seeds[4], (EXPERTS, D, FF), D ** -0.5, 0.125, ((0, 32), (2, 32))),
        "w_down": noise_with(seeds[5], (EXPERTS, FF, D), FF ** -0.5, 0.125, ((0, 32), (1, 32)), (1, 2, 32, 2.75)),
    }


def expert_block(operands):
    rows_in, gate_mat, up_mat, down_mat = operands
    gate_pre = jnp.dot(rows_in, gate_mat, preferred_element_type=jnp.float32)
    up_pre = jnp.dot(rows_in, up_mat, preferred_element_type=jnp.float32)
    hidden = (jax.nn.silu(gate_pre) * up_pre).astype(jnp.bfloat16)
    return jnp.dot(hidden, down_mat, preferred_element_type=jnp.float32).astype(jnp.bfloat16)


def reference(tokens, expert_ids, w_router, w_gate, w_up, w_down):
    columns = TOKENS // TOK_COL
    onehot = (expert_ids[:, None] == jnp.arange(EXPERTS, dtype=jnp.int32)[None, :]).astype(jnp.int32)
    blocked = onehot.reshape(columns, TOK_COL, EXPERTS)
    ranking = jnp.cumsum(blocked, axis=1) - blocked
    slots = jnp.sum(ranking * blocked, axis=2).reshape(TOKENS).astype(jnp.int32)
    column = (jnp.arange(TOKENS, dtype=jnp.int32) // TOK_COL).astype(jnp.int32)
    target = (expert_ids * (columns * CAP) + column * CAP + slots).astype(jnp.int32)
    buffers = jnp.zeros((EXPERTS * columns * CAP, D), jnp.bfloat16).at[target].set(tokens)
    buffers = buffers.reshape(EXPERTS, columns * CAP, D)
    results = lax.map(expert_block, (buffers, w_gate, w_up, w_down))
    expert_out = results.reshape(EXPERTS * columns * CAP, D)[target]
    router_logits = jnp.dot(tokens, w_router, preferred_element_type=jnp.float32)
    gating = jax.nn.sigmoid(jnp.sum(router_logits * onehot.astype(jnp.float32), axis=1))
    return (gating[:, None] * expert_out.astype(jnp.float32)).astype(jnp.bfloat16)
```

```python
import functools

import jax
import jax.numpy as jnp
from jax import lax
from jax.experimental import pallas as pl
from jax.experimental.pallas import tpu as pltpu
from jax.sharding import PartitionSpec as P

MESH = pl.DeviceIdType.MESH
CAP = 12
PAD = 16
RING = 8
BLOCKS = 3
PER = CAP // BLOCKS
F32 = jnp.float32
BF16 = jnp.bfloat16
NN = (((1,), (0,)), ((), ()))
NT = (((1,), (1,)), ((), ()))


def dot(a, b, dims=NN):
    return lax.dot_general(a, b, dims, preferred_element_type=F32)


def iota(shape, axis):
    return lax.broadcasted_iota(jnp.int32, shape, axis)


def kernel(
    ring, zs, es,
    ids_ref, tok_hbm, wr_hbm, wg_hbm, wu_hbm, wd_hbm, out_ref,
    tok, wr, wg, wu, wd, wdt, outg, inc, xb, gacc, uacc, hid,
    rs_out, rs_in, z_own, z_out, z_in, fin, r_out, r_in, placed_t, gate_col,
    load_sem, a_send, a_recv, ag_send, ag_recv, rs_send, rs_recv, z_send, z_recv, b_send, b_recv,
):
    me_dp = lax.axis_index("dp")
    me = lax.axis_index("expert")
    zl = me_dp // ring
    x = me_dp % ring
    half = ring // 2
    toks, width = tok.shape
    chunk = width // ring
    hidden = wg.shape[1]
    cols = width // (ring * zs)
    rows = es * PER
    slots = es * PAD

    loads = [
        pltpu.make_async_copy(src, dst, load_sem.at[i])
        for i, (src, dst) in enumerate(
            ((tok_hbm, tok), (wg_hbm, wg), (wu_hbm, wu), (wd_hbm, wd), (wr_hbm, wr))
        )
    ]
    for load in loads:
        load.start()

    right = zl * ring + (x + 1) % ring
    left = zl * ring + (x + ring - 1) % ring
    sides = (right, left)

    barrier = pltpu.get_barrier_semaphore()

    @pl.loop(1, es)
    def _(k):
        pl.semaphore_signal(barrier, inc=1, device_id={"expert": (me + k) % es}, device_id_type=MESH)

    for side in sides:
        pl.semaphore_signal(barrier, inc=1, device_id={"dp": side}, device_id_type=MESH)
    for k in range(1, zs):
        pl.semaphore_signal(
            barrier, inc=1, device_id={"dp": ((zl + k) % zs) * ring + x}, device_id_type=MESH
        )

    ids = ids_ref[...]
    onehot = (iota((es, toks), 0) == ids).astype(F32)
    before = (iota((toks, toks), 0) < iota((toks, toks), 1)).astype(BF16)
    rank = jnp.sum(dot(onehot.astype(BF16), before) * onehot, axis=0, keepdims=True)
    target = ((ids - me + es) % es) * PAD + rank.astype(jnp.int32)
    placing = (iota((slots, toks), 0) == target).astype(F32)

    loads[0].wait()
    mine = tok[:, pl.ds(pl.multiple_of(x * chunk, chunk), chunk)]
    sent = dot(placing.astype(BF16), mine).astype(BF16)
    outg[...] = sent.reshape(es, PAD, chunk)
    inc[0] = outg[0]

    pl.semaphore_wait(barrier, es - 1 + 2 + zs - 1)

    def dispatch(k):
        return pltpu.make_async_remote_copy(
            src_ref=outg.at[k], dst_ref=inc.at[k], send_sem=a_send, recv_sem=a_recv,
            device_id={"expert": (me + k) % es}, device_id_type=MESH,
        )

    @pl.loop(1, es)
    def _(k):
        dispatch(k).start()

    placed_t[...] = placing.T.astype(BF16)
    loads[4].wait()
    router = dot(tok[...], wr[...])
    picked = jnp.sum(router * onehot.T, axis=1, keepdims=True)
    gate_col[...] = jnp.broadcast_to(jax.nn.sigmoid(picked), gate_col.shape)
    loads[3].wait()
    for t in range(ring):
        for z in range(zs):
            start = (z * ring + t) * cols
            lo = start // 128 * 128
            tile = wd[:, lo:lo + 128].astype(F32).T
            wdt[t, z * cols:(z + 1) * cols, :] = tile[start - lo:start - lo + cols].astype(BF16)

    every = pl.ds(1, es - 1)
    pltpu.make_async_copy(inc.at[every], inc.at[every], a_recv).wait()

    def expand(b):
        i, r = iota((slots, rows), 0), iota((slots, rows), 1)
        return ((i // PAD == r // PER) & (i % PAD - b * PER == r % PER)).astype(BF16)

    def compact(b):
        r, i = iota((rows, slots), 0), iota((rows, slots), 1)
        return ((i // PAD == r // PER) & (i % PAD - b * PER == r % PER)).astype(BF16)

    def ag_hops(b):
        return (half, half - 1) if b % 2 == 0 else (half - 1, half)

    def rs_hops(b):
        return (half, half - 1) if b == 0 else (half - 1, half)

    def slot(way, step):
        return 0 if step == 0 else step + way * half

    def gather(way, step, b):
        return pltpu.make_async_remote_copy(
            src_ref=xb.at[slot(way, step - 1), b], dst_ref=xb.at[slot(way, step), b],
            send_sem=ag_send.at[way, step - 1, b], recv_sem=ag_recv.at[way, step - 1, b],
            device_id={"dp": sides[way]}, device_id_type=MESH,
        )

    def add_chunk(b, at, origin):
        block = xb[at, b]
        depth = pl.ds(pl.multiple_of(origin * chunk, chunk), chunk)
        g = dot(block, wg[depth, :])
        u = dot(block, wu[depth, :])
        if at == 0:
            gacc[b] = g
            uacc[b] = u
        else:
            gacc[b] += g
            uacc[b] += u

    packed = inc[...].reshape(slots, chunk)
    for b in range(BLOCKS):
        xb[0, b] = dot(compact(b), packed).astype(BF16)
        for way in range(2):
            gather(way, 1, b).start()
    loads[1].wait()
    loads[2].wait()
    for b in range(BLOCKS):
        add_chunk(b, 0, x)
    for step in range(1, half + 1):
        for b in range(BLOCKS):
            for way in range(2):
                hops = ag_hops(b)[way]
                if step > hops:
                    continue
                gather(way, step, b).wait_recv()
                if step < hops:
                    gather(way, step + 1, b).start()
                origin = (x + ring - step) % ring if way == 0 else (x + step) % ring
                add_chunk(b, slot(way, step), origin)

    def scatter(way, step, b):
        return pltpu.make_async_remote_copy(
            src_ref=rs_out.at[way, step - 1, b], dst_ref=rs_in.at[way, step - 1, b],
            send_sem=rs_send.at[way, step - 1, b], recv_sem=rs_recv.at[way, step - 1, b],
            device_id={"dp": sides[way]}, device_id_type=MESH,
        )

    def partial(b, t):
        return dot(wdt[t], hid[b], NT)

    def toward(way, distance):
        return (x + distance) % ring if way == 0 else (x + ring - distance) % ring

    for b in range(BLOCKS):
        g = gacc[b]
        hid[b] = (g / (1.0 + jnp.exp(-g)) * uacc[b]).astype(BF16)
        for way in range(2):
            rs_out[way, 0, b] = partial(b, toward(way, rs_hops(b)[way])).astype(BF16)
            scatter(way, 1, b).start()
    for step in range(2, half + 1):
        for b in range(BLOCKS):
            for way in range(2):
                hops = rs_hops(b)[way]
                if step > hops:
                    continue
                own = partial(b, toward(way, hops - step + 1))
                scatter(way, step - 1, b).wait_recv()
                rs_out[way, step - 1, b] = (own + rs_in[way, step - 2, b].astype(F32)).astype(BF16)
                scatter(way, step, b).start()

    def across(k, b):
        return pltpu.make_async_remote_copy(
            src_ref=z_out.at[b, (zl + k) % zs], dst_ref=z_in.at[b, k - 1],
            send_sem=z_send.at[k - 1, b], recv_sem=z_recv.at[k - 1, b],
            device_id={"dp": ((zl + k) % zs) * ring + x}, device_id_type=MESH,
        )

    for b in range(BLOCKS):
        total = partial(b, x)
        for way in range(2):
            hops = rs_hops(b)[way]
            scatter(way, hops, b).wait_recv()
            total = total + rs_in[way, hops - 1, b].astype(F32)
        total = total.reshape(zs, cols, rows)
        z_own[b] = total
        z_out[b] = total.astype(BF16)
        for k in range(1, zs):
            across(k, b).start()

    back = jnp.zeros((slots, 128), F32)
    for b in range(BLOCKS):
        total = z_own[b, zl]
        for k in range(1, zs):
            across(k, b).wait_recv()
            total = total + z_in[b, k - 1].astype(F32)
        fin[0:cols] = total.astype(BF16)
        if cols < 128:
            fin[cols:128] = jnp.zeros((128 - cols, rows), BF16)
        back = back + dot(expand(b), fin[...], NT)
    r_out[...] = back.astype(BF16).reshape(es, PAD, 128)
    r_in[0] = r_out[0]

    def give_back(k):
        return pltpu.make_async_remote_copy(
            src_ref=r_out.at[k], dst_ref=r_in.at[k], send_sem=b_send, recv_sem=b_recv,
            device_id={"expert": (me + es - k) % es}, device_id_type=MESH,
        )

    @pl.loop(1, es)
    def _(k):
        give_back(k).start()

    pltpu.make_async_copy(outg.at[every], outg.at[every], a_send).wait()
    for b in range(BLOCKS):
        for way in range(2):
            for step in range(1, ag_hops(b)[way] + 1):
                gather(way, step, b).wait_send()
            for step in range(1, rs_hops(b)[way] + 1):
                scatter(way, step, b).wait_send()
        for k in range(1, zs):
            across(k, b).wait_send()

    pltpu.make_async_copy(r_in.at[every], r_in.at[every], b_recv).wait()
    found = dot(placed_t[...], r_in[...].reshape(slots, 128))
    out_ref[...] = (gate_col[...] * found)[:, :cols].astype(BF16)
    pltpu.make_async_copy(r_out.at[every], r_out.at[every], b_send).wait()


def per_device(ring, zs, es, tokens, expert_ids, w_router, w_gate, w_up, w_down):
    toks, width = tokens.shape
    hidden = w_gate.shape[2]
    chunk = width // ring
    cols = width // (ring * zs)
    rows = es * PER
    half = ring // 2
    any_space = pl.BlockSpec(memory_space=pl.ANY)
    vmem = pl.BlockSpec(memory_space=pltpu.VMEM)
    dma = pltpu.SemaphoreType.DMA
    return pl.pallas_call(
        functools.partial(kernel, ring, zs, es),
        out_shape=jax.ShapeDtypeStruct((toks, cols), BF16),
        in_specs=[vmem] + [any_space] * 5,
        out_specs=vmem,
        scratch_shapes=[
            pltpu.VMEM((toks, width), BF16),
            pltpu.VMEM(w_router.shape, BF16),
            pltpu.VMEM((width, hidden), BF16),
            pltpu.VMEM((width, hidden), BF16),
            pltpu.VMEM((hidden, width), BF16),
            pltpu.VMEM((ring, zs * cols, hidden), BF16),
            pltpu.VMEM((es, PAD, chunk), BF16),
            pltpu.VMEM((es, PAD, chunk), BF16),
            pltpu.VMEM((ring + 1, BLOCKS, rows, chunk), BF16),
            pltpu.VMEM((BLOCKS, rows, hidden), F32),
            pltpu.VMEM((BLOCKS, rows, hidden), F32),
            pltpu.VMEM((BLOCKS, rows, hidden), BF16),
            pltpu.VMEM((2, half, BLOCKS, zs * cols, rows), BF16),
            pltpu.VMEM((2, half, BLOCKS, zs * cols, rows), BF16),
            pltpu.VMEM((BLOCKS, zs, cols, rows), F32),
            pltpu.VMEM((BLOCKS, zs, cols, rows), BF16),
            pltpu.VMEM((BLOCKS, max(zs - 1, 1), cols, rows), BF16),
            pltpu.VMEM((128, rows), BF16),
            pltpu.VMEM((es, PAD, 128), BF16),
            pltpu.VMEM((es, PAD, 128), BF16),
            pltpu.VMEM((toks, es * PAD), BF16),
            pltpu.VMEM((toks, 128), F32),
            dma((5,)),
            dma, dma,
            dma((2, half, BLOCKS)), dma((2, half, BLOCKS)),
            dma((2, half, BLOCKS)), dma((2, half, BLOCKS)),
            dma((max(zs - 1, 1), BLOCKS)), dma((max(zs - 1, 1), BLOCKS)),
            dma, dma,
        ],
        compiler_params=pltpu.CompilerParams(
            collective_id=0, has_side_effects=True, vmem_limit_bytes=56 * 2**20
        ),
        cost_estimate=pl.CostEstimate(
            flops=6 * BLOCKS * rows * width * hidden, bytes_accessed=6 * width * hidden, transcendentals=0
        ),
    )(
        expert_ids.reshape(1, toks), tokens, w_router, w_gate.reshape(width, hidden),
        w_up.reshape(width, hidden), w_down.reshape(hidden, width),
    )


def solution(mesh):
    es = mesh.shape["expert"]
    zs = mesh.shape["dp"] // RING
    in_specs = (
        P("expert", None),
        P("expert"),
        P(),
        P("expert", None, "dp"),
        P("expert", None, "dp"),
        P("expert", "dp", None),
    )
    return jax.shard_map(
        functools.partial(per_device, RING, zs, es), mesh=mesh, in_specs=in_specs,
        out_specs=P("expert", "dp"), check_vma=False,
    )
```

```python
import functools

import jax
import jax.numpy as jnp
from jax import lax
from jax.experimental import pallas as pl
from jax.experimental.pallas import tpu as pltpu
from jax.sharding import PartitionSpec as P

MESH = pl.DeviceIdType.MESH
CAP = 12
PAD = 16
RING = 8
GROUP = 8
LANES = 128
F32 = jnp.float32
BF16 = jnp.bfloat16
NN = (((1,), (0,)), ((), ()))
NT = (((1,), (1,)), ((), ()))


def dot(a, b, dims=NN):
    return lax.dot_general(a, b, dims, preferred_element_type=F32)


def iota(shape, axis):
    return lax.broadcasted_iota(jnp.int32, shape, axis)


def kernel(
    ring, zs, es,
    ids_hbm, tok_hbm, wr_hbm, wg_hbm, wu_hbm, wd_hbm, out_ref,
    ids_ref, own_tok, tok, wr, wg, wu, wd, wdt, outg, inc, xb, gacc, uacc, hid,
    rs_out, rs_in, z_own, z_out, z_in, fin, r_out, r_in, gate_row, placed, pick,
    load_sem, a_send, a_recv, ag_send, ag_recv, rs_send, rs_recv, z_send, z_recv, b_send, b_recv,
):
    me_dp = lax.axis_index("dp")
    me = lax.axis_index("expert")
    zl = me_dp // ring
    x = me_dp % ring
    half = ring // 2
    toks, width = tok.shape
    chunk = width // ring
    cols = width // (ring * zs)
    slots = es * PAD
    groups = es // GROUP
    grows = GROUP * CAP
    gslots = GROUP * PAD
    blocks = es * CAP // LANES
    far = ring - 1
    mine = pl.ds(pl.multiple_of(x * chunk, chunk), chunk)
    across_x = (x + half) % ring
    theirs = pl.ds(pl.multiple_of(across_x * chunk, chunk), chunk)

    loads = [
        pltpu.make_async_copy(src, dst, load_sem.at[i])
        for i, (src, dst) in enumerate((
            (tok_hbm.at[:, mine], own_tok), (tok_hbm, tok), (wr_hbm, wr),
            (wd_hbm, wd), (wg_hbm, wg), (wu_hbm, wu), (ids_hbm, ids_ref),
        ))
    ]
    for i in (6, 0, 1, 3, 4, 5, 2):
        loads[i].start()

    sides = (zl * ring + (x + 1) % ring, zl * ring + (x + ring - 1) % ring)
    barrier = pltpu.get_barrier_semaphore()

    @pl.loop(1, es)
    def _(k):
        pl.semaphore_signal(barrier, inc=1, device_id={"expert": me ^ k}, device_id_type=MESH)

    for side in sides:
        pl.semaphore_signal(barrier, inc=1, device_id={"dp": side}, device_id_type=MESH)
    for k in range(1, zs):
        pl.semaphore_signal(
            barrier, inc=1, device_id={"dp": ((zl + k) % zs) * ring + x}, device_id_type=MESH
        )

    loads[6].wait()
    ids = ids_ref[...]
    onehot = (iota((es, toks), 0) == ids).astype(F32)
    before = (iota((toks, toks), 0) < iota((toks, toks), 1)).astype(BF16)
    rank = jnp.sum(dot(onehot.astype(BF16), before) * onehot, axis=0, keepdims=True)
    target = (ids ^ me) * PAD + rank.astype(jnp.int32)
    placing = (iota((slots, toks), 0) == target).astype(F32)
    placed[...] = placing.astype(BF16)

    loads[0].wait()
    outg[0] = dot(placed[...], own_tok[...]).astype(BF16).reshape(es, PAD, chunk)

    pl.semaphore_wait(barrier, es - 1 + 2 + zs - 1)

    def dispatch(which, g, k):
        return pltpu.make_async_remote_copy(
            src_ref=outg.at[which, k], dst_ref=inc.at[which, k],
            send_sem=a_send.at[which, g], recv_sem=a_recv.at[which, g],
            device_id={"expert": me ^ k}, device_id_type=MESH,
        )

    def send_group(which, g):
        @pl.loop(max(g * GROUP, 1), (g + 1) * GROUP)
        def _(k):
            dispatch(which, g, k).start()

    def group_bytes(ref, which, g, sem):
        part = ref.at[which, pl.ds(max(g * GROUP, 1), GROUP - (g == 0))]
        return pltpu.make_async_copy(part, part, sem.at[which, g])

    for g in range(groups):
        send_group(0, g)

    inc[0, 0] = outg[0, 0]
    loads[1].wait()
    outg[1] = dot(placed[...], tok[:, theirs]).astype(BF16).reshape(es, PAD, chunk)
    inc[1, 0] = outg[1, 0]

    def spread(shape, source_axis):
        i, r = iota(shape, source_axis), iota(shape, 1 - source_axis)
        rank_at = i & (PAD - 1)
        return ((lax.shift_right_logical(i, 4) * CAP + rank_at == r) & (rank_at < CAP)).astype(BF16)

    compact = spread((grows, gslots), 1)
    pick[...] = spread(pick.shape, 0)

    def slot(way, step):
        return 0 if step == 0 else step + way * (half - 1)

    def gather(way, step, g):
        return pltpu.make_async_remote_copy(
            src_ref=xb.at[slot(way, step - 1), g], dst_ref=xb.at[slot(way, step), g],
            send_sem=ag_send.at[way, step - 1, g], recv_sem=ag_recv.at[way, step - 1, g],
            device_id={"dp": sides[way]}, device_id_type=MESH,
        )

    def arrived(which, at, g):
        group_bytes(inc, which, g, a_recv).wait()
        part = inc[which, g * GROUP:(g + 1) * GROUP].reshape(gslots, chunk)
        xb[at, g] = dot(compact, part).astype(BF16)

    def add_chunk(g, at, origin):
        block = xb[at, g]
        depth = pl.ds(pl.multiple_of(origin * chunk, chunk), chunk)
        gate = dot(block, wg[depth, :])
        up = dot(block, wu[depth, :])
        span = slice(g * grows, (g + 1) * grows)
        if at == 0:
            gacc[span] = gate
            uacc[span] = up
        else:
            gacc[span] += gate
            uacc[span] += up

    def rs_hops(b):
        return (half, half - 1) if b % 2 == 0 else (half - 1, half)

    def scatter(way, step, b):
        return pltpu.make_async_remote_copy(
            src_ref=rs_out.at[way, step - 1, b], dst_ref=rs_in.at[way, step - 1, b],
            send_sem=rs_send.at[way, step - 1, b], recv_sem=rs_recv.at[way, step - 1, b],
            device_id={"dp": sides[way]}, device_id_type=MESH,
        )

    def partial(b, t):
        return dot(wdt[t], hid[b], NT)

    def toward(way, distance):
        return (x + distance) % ring if way == 0 else (x + ring - distance) % ring

    def arrive(g):
        arrived(0, 0, g)
        for way in range(2):
            gather(way, 1, g).start()

    def hop(step, g):
        for way in range(2):
            gather(way, step, g).wait_recv()
            if step < half - 1:
                gather(way, step + 1, g).start()
            origin = (x + ring - step) % ring if way == 0 else (x + step) % ring
            add_chunk(g, slot(way, step), origin)

    def opposite(g):
        arrived(1, far, g)
        add_chunk(g, far, across_x)

    def begin_sums(b):
        gate = gacc[b * LANES:(b + 1) * LANES]
        up = uacc[b * LANES:(b + 1) * LANES]
        hid[b] = (gate / (1.0 + jnp.exp(-gate)) * up).astype(BF16)
        for way in range(2):
            rs_out[way, 0, b] = partial(b, toward(way, rs_hops(b)[way])).astype(BF16)
            scatter(way, 1, b).start()

    def send_opposite():
        for g in range(groups):
            send_group(1, g)

    def prepare():
        loads[3].wait()
        for t in range(ring):
            for z in range(zs):
                start = (z * ring + t) * cols
                lo = start // 128 * 128
                tile = wd[:, lo:lo + 128].astype(F32).T
                wdt[t, z * cols:(z + 1) * cols, :] = tile[start - lo:start - lo + cols].astype(BF16)

    def own_chunk(g):
        if g == 0:
            loads[4].wait()
            loads[5].wait()
        add_chunk(g, 0, x)

    steps = [(half - 2.8, 0, send_opposite, ()), (half - 2.4, 0, prepare, ())]
    for g in range(groups):
        late = 0 if 2 * g < groups else 1.5
        steps.append((late, g, arrive, (g,)))
        steps.append((late + 0.1, g, own_chunk, (g,)))
        for step in range(1, half):
            steps.append((late + step, g, hop, (step, g)))
        steps.append((late + half - 1.4, g, opposite, (g,)))
    for b in range(blocks):
        last = ((b + 1) * LANES - 1) // grows
        late = 0 if 2 * last < groups else 1.5
        steps.append((late + half - 0.9, b, begin_sums, (b,)))
    for _, _, action, given in sorted(steps, key=lambda entry: entry[:2]):
        action(*given)

    loads[2].wait()
    router = dot(wr[...], tok[...], NT)
    picked = jnp.sum(router * (iota((es, toks), 0) == ids_ref[...]).astype(F32), axis=0, keepdims=True)
    gate_row[...] = jnp.broadcast_to(jax.nn.sigmoid(picked), gate_row.shape)

    for step in range(2, half + 1):
        for b in range(blocks):
            for way in range(2):
                hops = rs_hops(b)[way]
                if step > hops:
                    continue
                own = partial(b, toward(way, hops - step + 1))
                scatter(way, step - 1, b).wait_recv()
                rs_out[way, step - 1, b] = (own + rs_in[way, step - 2, b].astype(F32)).astype(BF16)
                scatter(way, step, b).start()

    def across(k, b):
        return pltpu.make_async_remote_copy(
            src_ref=z_out.at[b, (zl + k) % zs], dst_ref=z_in.at[b, k - 1],
            send_sem=z_send.at[k - 1, b], recv_sem=z_recv.at[k - 1, b],
            device_id={"dp": ((zl + k) % zs) * ring + x}, device_id_type=MESH,
        )

    for b in range(blocks):
        total = partial(b, x)
        for way in range(2):
            hops = rs_hops(b)[way]
            scatter(way, hops, b).wait_recv()
            total = total + rs_in[way, hops - 1, b].astype(F32)
        total = total.reshape(zs, cols, LANES)
        z_out[b] = total.astype(BF16)
        for k in range(1, zs):
            across(k, b).start()
        z_own[b] = total

    def give_back(k):
        return pltpu.make_async_remote_copy(
            src_ref=r_out.at[k], dst_ref=r_in.at[k], send_sem=b_send, recv_sem=b_recv,
            device_id={"expert": me ^ k}, device_id_type=MESH,
        )

    fin[...] = jnp.zeros_like(fin)
    first = 0
    for b in range(blocks):
        total = z_own[b, zl]
        for k in range(1, zs):
            across(k, b).wait_recv()
            total = total + z_in[b, k - 1].astype(F32)
        fin[b, 0:cols] = total.astype(BF16)
        last = (b + 1) * LANES // CAP
        back = jnp.zeros(((last - first) * PAD, 128), F32)
        for c in range(first * CAP // LANES, b + 1):
            part = pick[first * PAD:last * PAD, c * LANES:(c + 1) * LANES]
            back = back + dot(part, fin[c], NT)
        r_out[first:last] = back.astype(BF16).reshape(last - first, PAD, 128)

        @pl.loop(max(first, 1), last)
        def _(k):
            give_back(k).start()

        first = last

    r_in[0] = r_out[0]
    for which in range(2):
        for g in range(groups):
            group_bytes(outg, which, g, a_send).wait()
    for way in range(2):
        for step in range(1, half):
            for g in range(groups):
                gather(way, step, g).wait_send()
        for b in range(blocks):
            for step in range(1, rs_hops(b)[way] + 1):
                scatter(way, step, b).wait_send()
    for b in range(blocks):
        for k in range(1, zs):
            across(k, b).wait_send()

    every = pl.ds(1, es - 1)
    pltpu.make_async_copy(r_in.at[every], r_in.at[every], b_recv).wait()
    back = r_in[...].reshape(slots, 128)
    found = lax.dot_general(placed[...], back, (((0,), (0,)), ((), ())), preferred_element_type=F32)
    out_ref[...] = (gate_row[0:1] * found.T[:cols]).astype(BF16)
    pltpu.make_async_copy(r_out.at[every], r_out.at[every], b_send).wait()


def per_device(ring, zs, es, tokens, expert_ids, w_router, w_gate, w_up, w_down):
    toks, width = tokens.shape
    hidden = w_gate.shape[2]
    chunk = width // ring
    cols = width // (ring * zs)
    half = ring // 2
    rows = es * CAP
    groups = es // GROUP
    blocks = rows // LANES
    zn = max(zs - 1, 1)
    any_space = pl.BlockSpec(memory_space=pl.ANY)
    vmem = pl.BlockSpec(memory_space=pltpu.VMEM)
    dma = pltpu.SemaphoreType.DMA
    out = pl.pallas_call(
        functools.partial(kernel, ring, zs, es),
        out_shape=jax.ShapeDtypeStruct((cols, toks), BF16),
        in_specs=[any_space] * 6,
        out_specs=vmem,
        scratch_shapes=[
            pltpu.VMEM((1, toks), jnp.int32),
            pltpu.VMEM((toks, chunk), BF16),
            pltpu.VMEM((toks, width), BF16),
            pltpu.VMEM((es, width), BF16),
            pltpu.VMEM((width, hidden), BF16),
            pltpu.VMEM((width, hidden), BF16),
            pltpu.VMEM((hidden, width), BF16),
            pltpu.VMEM((ring, zs * cols, hidden), BF16),
            pltpu.VMEM((2, es, PAD, chunk), BF16),
            pltpu.VMEM((2, es, PAD, chunk), BF16),
            pltpu.VMEM((ring, groups, GROUP * CAP, chunk), BF16),
            pltpu.VMEM((rows, hidden), F32),
            pltpu.VMEM((rows, hidden), F32),
            pltpu.VMEM((blocks, LANES, hidden), BF16),
            pltpu.VMEM((2, half, blocks, zs * cols, LANES), BF16),
            pltpu.VMEM((2, half, blocks, zs * cols, LANES), BF16),
            pltpu.VMEM((blocks, zs, cols, LANES), F32),
            pltpu.VMEM((blocks, zs, cols, LANES), BF16),
            pltpu.VMEM((blocks, zn, cols, LANES), BF16),
            pltpu.VMEM((blocks, 128, LANES), BF16),
            pltpu.VMEM((es, PAD, 128), BF16),
            pltpu.VMEM((es, PAD, 128), BF16),
            pltpu.VMEM((8, toks), F32),
            pltpu.VMEM((es * PAD, toks), BF16),
            pltpu.VMEM((es * PAD, rows), BF16),
            dma((7,)),
            dma((2, groups)), dma((2, groups)),
            dma((2, half - 1, groups)), dma((2, half - 1, groups)),
            dma((2, half, blocks)), dma((2, half, blocks)),
            dma((zn, blocks)), dma((zn, blocks)),
            dma, dma,
        ],
        compiler_params=pltpu.CompilerParams(
            collective_id=0, has_side_effects=True, vmem_limit_bytes=56 * 2**20
        ),
        cost_estimate=pl.CostEstimate(
            flops=6 * rows * width * hidden, bytes_accessed=6 * width * hidden, transcendentals=0
        ),
    )(
        expert_ids.reshape(1, toks), tokens, w_router.T, w_gate.reshape(width, hidden),
        w_up.reshape(width, hidden), w_down.reshape(hidden, width),
    )
    return out.T


def solution(mesh):
    es = mesh.shape["expert"]
    zs = mesh.shape["dp"] // RING
    in_specs = (
        P("expert", None),
        P("expert"),
        P(),
        P("expert", None, "dp"),
        P("expert", None, "dp"),
        P("expert", "dp", None),
    )
    return jax.shard_map(
        functools.partial(per_device, RING, zs, es), mesh=mesh, in_specs=in_specs,
        out_specs=P("expert", "dp"), check_vma=False,
    )
```

```python
import functools

import jax
import jax.numpy as jnp
from jax import lax
from jax.experimental import pallas as pl
from jax.experimental.pallas import tpu as pltpu
from jax.sharding import PartitionSpec as P

MESH = pl.DeviceIdType.MESH
CAP = 12
PAD = 16
RING = 8
GROUP = 8
LANES = 384
F32 = jnp.float32
BF16 = jnp.bfloat16
NN = (((1,), (0,)), ((), ()))
NT = (((1,), (1,)), ((), ()))


def dot(a, b, dims=NN):
    return lax.dot_general(a, b, dims, preferred_element_type=F32)


def iota(shape, axis):
    return lax.broadcasted_iota(jnp.int32, shape, axis)


def kernel(
    ring, zs, es,
    ids_hbm, tok_hbm, wr_hbm, wg_hbm, wu_hbm, wd_hbm, out_ref,
    ids_ref, own_tok, tok, wr, wg, wu, wd, wdt, outg, inc, xb, gacc, uacc, hid,
    rs_out, rs_in, z_own, z_out, z_in, fin, r_out, r_in, gate_row, placed, placed_t, pick,
    load_sem, a_send, a_recv, ag_send, ag_recv, rs_send, rs_recv, z_send, z_recv, b_send, b_recv,
):
    me_dp = lax.axis_index("dp")
    me = lax.axis_index("expert")
    zl = me_dp // ring
    x = me_dp % ring
    half = ring // 2
    toks, width = tok.shape
    chunk = width // ring
    cols = width // (ring * zs)
    slots = es * PAD
    groups = es // GROUP
    grows = GROUP * CAP
    gslots = GROUP * PAD
    blocks = es * CAP // LANES
    far = ring - 1
    mine = pl.ds(pl.multiple_of(x * chunk, chunk), chunk)
    across_x = (x + half) % ring
    theirs = pl.ds(pl.multiple_of(across_x * chunk, chunk), chunk)

    loads = [
        pltpu.make_async_copy(src, dst, load_sem.at[i])
        for i, (src, dst) in enumerate((
            (tok_hbm.at[:, mine], own_tok), (tok_hbm, tok), (wr_hbm, wr),
            (wd_hbm, wd), (wg_hbm, wg), (wu_hbm, wu), (ids_hbm, ids_ref),
        ))
    ]
    for i in (6, 0, 1, 3, 4, 5, 2):
        loads[i].start()

    sides = (zl * ring + (x + 1) % ring, zl * ring + (x + ring - 1) % ring)
    barrier = pltpu.get_barrier_semaphore()

    @pl.loop(1, es)
    def _(k):
        pl.semaphore_signal(barrier, inc=1, device_id={"expert": me ^ k}, device_id_type=MESH)

    for side in sides:
        pl.semaphore_signal(barrier, inc=1, device_id={"dp": side}, device_id_type=MESH)
    for k in range(1, zs):
        pl.semaphore_signal(
            barrier, inc=1, device_id={"dp": ((zl + k) % zs) * ring + x}, device_id_type=MESH
        )

    loads[6].wait()
    ids = ids_ref[...]
    onehot = (iota((es, toks), 0) == ids).astype(F32)
    before = (iota((toks, toks), 0) < iota((toks, toks), 1)).astype(BF16)
    rank = jnp.sum(dot(onehot.astype(BF16), before) * onehot, axis=0, keepdims=True)
    target = (ids ^ me) * PAD + rank.astype(jnp.int32)
    placing = (iota((slots, toks), 0) == target).astype(F32)
    placed[...] = placing.astype(BF16)

    loads[0].wait()
    outg[0] = dot(placed[...], own_tok[...]).astype(BF16).reshape(es, PAD, chunk)

    pl.semaphore_wait(barrier, es - 1 + 2 + zs - 1)

    def dispatch(which, g, k):
        return pltpu.make_async_remote_copy(
            src_ref=outg.at[which, k], dst_ref=inc.at[which, k],
            send_sem=a_send.at[which, g], recv_sem=a_recv.at[which, g],
            device_id={"expert": me ^ k}, device_id_type=MESH,
        )

    def send_group(which, g):
        @pl.loop(max(g * GROUP, 1), (g + 1) * GROUP)
        def _(k):
            dispatch(which, g, k).start()

    def group_bytes(ref, which, g, sem):
        part = ref.at[which, pl.ds(max(g * GROUP, 1), GROUP - (g == 0))]
        return pltpu.make_async_copy(part, part, sem.at[which, g])

    for g in range(groups):
        send_group(0, g)

    inc[0, 0] = outg[0, 0]
    loads[3].wait()
    for t in range(ring):
        for z in range(zs):
            start = (z * ring + t) * cols
            lo = start // 128 * 128
            tile = wd[:, lo:lo + 128].astype(F32).T
            wdt[t, z * cols:(z + 1) * cols, :] = tile[start - lo:start - lo + cols].astype(BF16)

    def spread(shape, source_axis):
        i, r = iota(shape, source_axis), iota(shape, 1 - source_axis)
        rank_at = i & (PAD - 1)
        return ((lax.shift_right_logical(i, 4) * CAP + rank_at == r) & (rank_at < CAP)).astype(BF16)

    compact = spread((grows, gslots), 1)

    def slot(way, step):
        return 0 if step == 0 else step + way * (half - 1)

    def gather(way, step, g):
        return pltpu.make_async_remote_copy(
            src_ref=xb.at[slot(way, step - 1), g], dst_ref=xb.at[slot(way, step), g],
            send_sem=ag_send.at[way, step - 1, g], recv_sem=ag_recv.at[way, step - 1, g],
            device_id={"dp": sides[way]}, device_id_type=MESH,
        )

    def arrived(which, at, g):
        group_bytes(inc, which, g, a_recv).wait()
        part = inc[which, g * GROUP:(g + 1) * GROUP].reshape(gslots, chunk)
        xb[at, g] = dot(compact, part).astype(BF16)

    def add_chunk(g, at, origin):
        block = xb[at, g]
        depth = pl.ds(pl.multiple_of(origin * chunk, chunk), chunk)
        gate = dot(block, wg[depth, :])
        up = dot(block, wu[depth, :])
        span = slice(g * grows, (g + 1) * grows)
        if at == 0:
            gacc[span] = gate
            uacc[span] = up
        else:
            gacc[span] += gate
            uacc[span] += up

    def rs_hops(b):
        return (half, half - 1) if b % 2 == 0 else (half - 1, half)

    def scatter(way, step, b):
        return pltpu.make_async_remote_copy(
            src_ref=rs_out.at[way, step - 1, b], dst_ref=rs_in.at[way, step - 1, b],
            send_sem=rs_send.at[way, step - 1, b], recv_sem=rs_recv.at[way, step - 1, b],
            device_id={"dp": sides[way]}, device_id_type=MESH,
        )

    def partial(b, t):
        return dot(wdt[t], hid[b], NT)

    def toward(way, distance):
        return (x + distance) % ring if way == 0 else (x + ring - distance) % ring

    def arrive(g):
        arrived(0, 0, g)
        for way in range(2):
            gather(way, 1, g).start()

    def hop(step, g):
        for way in range(2):
            gather(way, step, g).wait_recv()
            if step < half - 1:
                gather(way, step + 1, g).start()
            origin = (x + ring - step) % ring if way == 0 else (x + step) % ring
            add_chunk(g, slot(way, step), origin)

    def opposite(g):
        arrived(1, far, g)
        add_chunk(g, far, across_x)

    def begin_sums(b):
        gate = gacc[b * LANES:(b + 1) * LANES]
        up = uacc[b * LANES:(b + 1) * LANES]
        hid[b] = (gate / (1.0 + jnp.exp(-gate)) * up).astype(BF16)
        for way in range(2):
            rs_out[way, 0, b] = partial(b, toward(way, rs_hops(b)[way])).astype(BF16)
            scatter(way, 1, b).start()

    def send_opposite():
        loads[1].wait()
        outg[1] = dot(placed[...], tok[:, theirs]).astype(BF16).reshape(es, PAD, chunk)
        inc[1, 0] = outg[1, 0]
        for g in range(groups):
            send_group(1, g)

    def own_chunk(g):
        if g == 0:
            loads[4].wait()
            loads[5].wait()
        add_chunk(g, 0, x)

    def gates():
        loads[2].wait()
        router = dot(wr[...], tok[...], NT)
        chosen = (iota((es, toks), 0) == ids_ref[...]).astype(F32)
        picked = jnp.sum(router * chosen, axis=0, keepdims=True)
        gate_row[...] = jnp.broadcast_to(jax.nn.sigmoid(picked), gate_row.shape)
        placed_t[...] = placed[...].astype(F32).T.astype(BF16)
        pick[...] = spread(pick.shape, 0)
        fin[...] = jnp.zeros_like(fin)

    def sums(step, b):
        for way in range(2):
            hops = rs_hops(b)[way]
            if step > hops:
                continue
            own = partial(b, toward(way, hops - step + 1))
            scatter(way, step - 1, b).wait_recv()
            rs_out[way, step - 1, b] = (own + rs_in[way, step - 2, b].astype(F32)).astype(BF16)
            scatter(way, step, b).start()

    def across(k, b):
        return pltpu.make_async_remote_copy(
            src_ref=z_out.at[b, (zl + k) % zs], dst_ref=z_in.at[b, k - 1],
            send_sem=z_send.at[k - 1, b], recv_sem=z_recv.at[k - 1, b],
            device_id={"dp": ((zl + k) % zs) * ring + x}, device_id_type=MESH,
        )

    def finish(b):
        total = partial(b, x)
        for way in range(2):
            hops = rs_hops(b)[way]
            scatter(way, hops, b).wait_recv()
            total = total + rs_in[way, hops - 1, b].astype(F32)
        total = total.reshape(zs, cols, LANES)
        z_out[b] = total.astype(BF16)
        for k in range(1, zs):
            across(k, b).start()
        z_own[b] = total

    def give_back(k):
        return pltpu.make_async_remote_copy(
            src_ref=r_out.at[k], dst_ref=r_in.at[k], send_sem=b_send, recv_sem=b_recv,
            device_id={"expert": me ^ k}, device_id_type=MESH,
        )

    def close(b):
        total = z_own[b, zl]
        for k in range(1, zs):
            across(k, b).wait_recv()
            total = total + z_in[b, k - 1].astype(F32)
        fin[b, 0:cols] = total.astype(BF16)
        first = b * LANES // CAP
        last = (b + 1) * LANES // CAP
        back = jnp.zeros(((last - first) * PAD, 128), F32)
        for c in range(first * CAP // LANES, b + 1):
            part = pick[first * PAD:last * PAD, c * LANES:(c + 1) * LANES]
            back = back + dot(part, fin[c], NT)
        r_out[first:last] = back.astype(BF16).reshape(last - first, PAD, 128)

        @pl.loop(max(first, 1), last)
        def _(k):
            give_back(k).start()

    steps = [(half - 2.8, 0, send_opposite, ()), (half - 1.95, 0, gates, ())]
    for g in range(groups):
        late = 0 if 2 * g < groups else 1.5
        steps.append((late, g, arrive, (g,)))
        steps.append((late + 0.1, g, own_chunk, (g,)))
        for step in range(1, half):
            steps.append((late + step, g, hop, (step, g)))
        steps.append((late + half - 1.4, g, opposite, (g,)))
    for b in range(blocks):
        last = ((b + 1) * LANES - 1) // grows
        late = 0 if 2 * last < groups else 1.5
        base = late + half - 0.9
        steps.append((base, b, begin_sums, (b,)))
        for step in range(2, half + 1):
            steps.append((10 + step, b, sums, (step, b)))
        steps.append((20, b, finish, (b,)))
        steps.append((30, b, close, (b,)))
    for _, _, action, given in sorted(steps, key=lambda entry: entry[:2]):
        action(*given)

    r_in[0] = r_out[0]
    for which in range(2):
        for g in range(groups):
            group_bytes(outg, which, g, a_send).wait()
    for way in range(2):
        for step in range(1, half):
            for g in range(groups):
                gather(way, step, g).wait_send()
        for b in range(blocks):
            for step in range(1, rs_hops(b)[way] + 1):
                scatter(way, step, b).wait_send()
    for b in range(blocks):
        for k in range(1, zs):
            across(k, b).wait_send()

    every = pl.ds(1, es - 1)
    pltpu.make_async_copy(r_in.at[every], r_in.at[every], b_recv).wait()
    back = r_in[...].reshape(slots, 128)
    found = dot(placed_t[...], back)
    out_ref[...] = (gate_row[0:1] * found.T[:cols]).astype(BF16)
    pltpu.make_async_copy(r_out.at[every], r_out.at[every], b_send).wait()


def per_device(ring, zs, es, tokens, expert_ids, w_router, w_gate, w_up, w_down):
    toks, width = tokens.shape
    hidden = w_gate.shape[2]
    chunk = width // ring
    cols = width // (ring * zs)
    half = ring // 2
    rows = es * CAP
    groups = es // GROUP
    blocks = rows // LANES
    zn = max(zs - 1, 1)
    any_space = pl.BlockSpec(memory_space=pl.ANY)
    vmem = pl.BlockSpec(memory_space=pltpu.VMEM)
    dma = pltpu.SemaphoreType.DMA
    out = pl.pallas_call(
        functools.partial(kernel, ring, zs, es),
        out_shape=jax.ShapeDtypeStruct((cols, toks), BF16),
        in_specs=[any_space] * 6,
        out_specs=vmem,
        scratch_shapes=[
            pltpu.VMEM((1, toks), jnp.int32),
            pltpu.VMEM((toks, chunk), BF16),
            pltpu.VMEM((toks, width), BF16),
            pltpu.VMEM((es, width), BF16),
            pltpu.VMEM((width, hidden), BF16),
            pltpu.VMEM((width, hidden), BF16),
            pltpu.VMEM((hidden, width), BF16),
            pltpu.VMEM((ring, zs * cols, hidden), BF16),
            pltpu.VMEM((2, es, PAD, chunk), BF16),
            pltpu.VMEM((2, es, PAD, chunk), BF16),
            pltpu.VMEM((ring, groups, GROUP * CAP, chunk), BF16),
            pltpu.VMEM((rows, hidden), F32),
            pltpu.VMEM((rows, hidden), F32),
            pltpu.VMEM((blocks, LANES, hidden), BF16),
            pltpu.VMEM((2, half, blocks, zs * cols, LANES), BF16),
            pltpu.VMEM((2, half, blocks, zs * cols, LANES), BF16),
            pltpu.VMEM((blocks, zs, cols, LANES), F32),
            pltpu.VMEM((blocks, zs, cols, LANES), BF16),
            pltpu.VMEM((blocks, zn, cols, LANES), BF16),
            pltpu.VMEM((blocks, 128, LANES), BF16),
            pltpu.VMEM((es, PAD, 128), BF16),
            pltpu.VMEM((es, PAD, 128), BF16),
            pltpu.VMEM((8, toks), F32),
            pltpu.VMEM((es * PAD, toks), BF16),
            pltpu.VMEM((toks, es * PAD), BF16),
            pltpu.VMEM((es * PAD, rows), BF16),
            dma((7,)),
            dma((2, groups)), dma((2, groups)),
            dma((2, half - 1, groups)), dma((2, half - 1, groups)),
            dma((2, half, blocks)), dma((2, half, blocks)),
            dma((zn, blocks)), dma((zn, blocks)),
            dma, dma,
        ],
        compiler_params=pltpu.CompilerParams(
            collective_id=0, has_side_effects=True, vmem_limit_bytes=56 * 2**20
        ),
        cost_estimate=pl.CostEstimate(
            flops=6 * rows * width * hidden, bytes_accessed=6 * width * hidden, transcendentals=0
        ),
    )(
        expert_ids.reshape(1, toks), tokens, w_router.T, w_gate.reshape(width, hidden),
        w_up.reshape(width, hidden), w_down.reshape(hidden, width),
    )
    return out.T


def solution(mesh):
    es = mesh.shape["expert"]
    zs = mesh.shape["dp"] // RING
    in_specs = (
        P("expert", None),
        P("expert"),
        P(),
        P("expert", None, "dp"),
        P("expert", None, "dp"),
        P("expert", "dp", None),
    )
    return jax.shard_map(
        functools.partial(per_device, RING, zs, es), mesh=mesh, in_specs=in_specs,
        out_specs=P("expert", "dp"), check_vma=False,
    )
```
